32 devices in a mesh: groups: 2 (over y), rows: 2 (over x), expert: 4 (over z), pair: 2 (over core).
Axes of the slice: x: 2, y: 2, z: 4, core: 2. Of those that a mesh axis runs over, the one named last changes fastest.
Arguments:
- acts: bfloat16 [512, 6144], P(('groups', 'rows', 'expert'), 'pair'), parts along dimension 0, may hold values from -6 to 6
- grads: bfloat16 [512, 2, 16384], P(('groups', 'rows', 'expert'), None, 'pair'), parts along dimension 0, may hold values from -0.1796875 to 0.1796875
- routes: int32 [512, 2], P(('groups', 'rows', 'expert')), parts along dimension 0, may hold values from 0 to 3, all different within a row; in each aligned block of 32 rows (0 to 31, 32 to 63, ...) at most 24 rows name the same one
- seq_ids: int32 [512], P(('groups', 'rows', 'expert')), parts along dimension 0, may hold values from 0 to 3, never falling along the last dimension, each value on 1 to 96 neighbouring positions
- p_in: bfloat16 [4, 2, 3072, 64], P('expert', 'pair', 'rows'), may hold values from -0.078125 to 0.078125
- p_out: bfloat16 [4, 2, 8192, 64], P('expert', 'pair', 'rows'), may hold values from -0.046875 to 0.046875
Outputs:
- features: float32 [8, 4, 4096], P('groups', 'expert', ('rows', 'pair')), parts along dimension 0
The draws below stay inside these ranges and needn't reach their ends.
There are 2 independent parts, one for each index of `groups`. The reference program is written for one: setup_inputs(seed, part) draws one part's arguments, and reference() takes and returns one part's arrays. A program takes and returns all parts, laid end to end along the dimension named above; an argument that names none is the same for every part. Nothing has to cross between parts.
Inputs may be any that keep to these rules, and one draw needn't show every extreme that they name: `routes`: in the rows of one device (aligned blocks of 32 tokens) no expert is named by more than 24 entries, and in every draw some expert is named by exactly 24 entries in some block; a token never names one expert twice. `seq_ids`: never falling along the tokens; every sequence holds 1 to 96 tokens, one exactly that many.
All inputs are finite; a program needn't handle non-finite values.
Results may differ from the reference program's by a relative error of at most 0.0003.
Values may be sent and summed in bfloat16 or wider, within the bound.
A program may use at most 64 MiB of HBM per device.

```python
import math
import jax
import jax.numpy as jnp
import numpy as np
from jax import lax

D = 6144
FF = 16384
TOP = 2
K_IN = 64
K_OUT = 64
TOK_DEV = 32
SEQS = 4
EXPERTS = 4
TOKENS = 256
LEN = 64
CAP = 24
N_ROWS = 2
N_EXPERT = 4


def block_levels(key, shape, cuts, least, high):
    level = 1.0
    for position, shards_of in cuts:
        draws = jax.random.uniform(jax.random.fold_in(jax.random.fold_in(key, 6), position), (shards_of,), jnp.float32, least / len(cuts), high / len(cuts))
        level = level * jnp.repeat(jnp.exp(draws), shape[position] // shards_of).reshape((-1,) + (1,) * (len(shape) - 1 - position))
    return level


def profile(amount, total, limit, lean):
    weights = [(1 << 20) // math.isqrt(grade ** lean) + 1 for grade in range(2, amount + 1)]
    spare, holding = total - limit - (amount - 1), [1] * (amount - 1)
    while spare > 0:
        movable = [i for i in range(amount - 1) if holding[i] < limit]
        mass, remaining = sum([weights[i] for i in movable]), spare
        for i in movable:
            more = min(limit - holding[i], max(1, remaining * weights[i] // mass), spare)
            holding[i] = holding[i] + more
            spare = spare - more
    return np.array([limit] + holding)


def ragged(own_key, amount, total, reach, lean):
    if amount == 2:
        one = jax.random.randint(own_key, (), max(1, total - reach), min(reach, total - 1) + 1)
        return jnp.stack([one, total - one])
    tallies = jnp.asarray(profile(amount, total, reach, lean), jnp.int32)
    twos = (amount - 1) // 2
    donor, taker = tallies[1:1 + 2 * twos:2], tallies[2:2 + 2 * twos:2]
    room = jnp.minimum(donor - 1, reach - taker)
    moved = jax.random.randint(jax.random.fold_in(own_key, 1), (twos,), 0, 1 << 20) % (room + 1)
    tallies = tallies.at[1:1 + 2 * twos:2].set(donor - moved).at[2:2 + 2 * twos:2].set(taker + moved)
    return tallies[jax.random.permutation(jax.random.fold_in(own_key, 2), amount)]


def shared_out(key, own, number, rows, amount, top, limit, lean):
    order = jax.random.permutation(key, amount)
    heavy_load, common = portions_of(amount, rows * top, limit, lean, True), portions_of(amount, rows * top, limit, lean, False)
    places = jnp.arange(amount)

    def named(sizes, rotation):
        used = int((sizes > 0).sum())
        fixed = max(1, used // 4)
        shifted = fixed + (places - fixed + rotation * (used - fixed)) % max(1, amount - fixed)
        return jnp.zeros((amount,), jnp.int32).at[order[jnp.where(places < fixed, places, shifted)]].set(jnp.asarray(sizes, jnp.int32))

    sizes = jnp.where(number % 4 == 0, named(heavy_load, number // 4), named(common, number - number // 4 - 1))
    mixed = jax.random.permutation(jax.random.fold_in(own, 3), amount)
    donor, taker = mixed[0:amount // 2 * 2:2], mixed[1:amount // 2 * 2:2]
    room = jnp.minimum(sizes[donor] - 1, limit - sizes[taker]) // 2
    room = jnp.where((donor == order[0]) | (taker == order[0]) | (sizes[taker] == 0), 0, jnp.maximum(room, 0))
    shifted = jax.random.randint(jax.random.fold_in(own, 4), (amount // 2,), 0, 1 << 20) % (room + 1)
    sizes = sizes.at[donor].add(-shifted).at[taker].add(shifted)
    items = jnp.searchsorted(jnp.cumsum(sizes), jnp.arange(rows * top), side="right").astype(jnp.int32)
    grid = items.reshape(top, rows).T
    grid = grid[jax.random.permutation(jax.random.fold_in(own, 1), rows)]
    rotation = jax.random.randint(jax.random.fold_in(own, 2), (rows, 1), 0, top)
    return jnp.take_along_axis(grid, (jnp.arange(top)[None, :] + rotation) % top, axis=1)


def portions_of(count, total, reach, skew, full):
    loads = [(1 << 20) // math.isqrt(rank ** skew) + 1 for rank in range(1, count + 1)]
    largest = reach if full else min(reach, max(-(-total // count), total * loads[0] // sum(loads)))
    least = 1 if total - largest >= count - 1 else 0
    counts, spare = [largest] + [least] * (count - 1), total - largest - least * (count - 1)
    while spare > 0:
        candidates = [i for i in range(1, count) if counts[i] < largest] or [i for i in range(1, count) if counts[i] < reach]
        pool, left = sum([loads[i] for i in candidates]), spare
        for i in candidates:
            extra = min(reach - counts[i], max(1, left * loads[i] // pool), spare)
            counts[i] = counts[i] + extra
            spare = spare - extra
    return np.array(counts)


def bell_draw(own_key, dims, scale, most, cuts=(), kind=jnp.bfloat16):
    factor_of = block_levels(own_key, dims, cuts, -0.22, 0.18) if cuts else 1.0
    result = jax.random.normal(own_key, dims, jnp.float32) * scale * factor_of
    return jnp.minimum(jnp.maximum(result, -most), most).astype(kind)


def setup_inputs(seed: int = 0, part: int = 0) -> dict:
    seeds = jax.random.split(jax.random.key(seed), 7)
    part_splits = jax.random.split(jax.random.fold_in(seeds[6], part), 7)
    acts = bell_draw(part_splits[0], (TOKENS, D), 1.0, 6.0, ((0, 8), (1, 2)))
    grads = bell_draw(part_splits[1], (TOKENS, TOP, FF), 0.03, 0.1796875, ((0, 8), (2, 2)))
    routes_keys = jax.random.split(jax.random.fold_in(part_splits[2], 1), TOKENS // TOK_DEV)
    routes_turns = jax.random.permutation(jax.random.fold_in(part_splits[2], 3), TOKENS // TOK_DEV)
    routes = jax.vmap(lambda own, number: shared_out(jax.random.fold_in(part_splits[2], 2), own, number, TOK_DEV, EXPERTS, TOP, CAP, 2))(routes_keys, routes_turns).reshape((TOKENS, TOP))
    seq_ids = jnp.searchsorted(jnp.cumsum(ragged(part_splits[3], SEQS, TOKENS, LEN + LEN // 2, 1)), jnp.arange(TOKENS), side="right").astype(jnp.int32)
    p_in = bell_draw(seeds[4], (EXPERTS, 2, D // 2, K_IN), D ** -0.5, 0.078125, ((0, 4), (1, 2), (2, 2)))
    p_out = bell_draw(seeds[5], (EXPERTS, 2, FF // 2, K_OUT), FF ** -0.5, 0.046875, ((0, 4), (1, 2), (2, 2)))
    return {"acts": acts, "grads": grads, "routes": routes, "seq_ids": seq_ids, "p_in": p_in, "p_out": p_out}


def reference(acts, grads, routes, seq_ids, p_in, p_out):
    tok = routes.shape[0]
    top = routes.shape[1]
    n_exp = p_in.shape[0]
    k_in = p_in.shape[3]
    k_out = p_out.shape[3]
    pin_all = p_in.reshape(n_exp, D, k_in)
    pout_all = p_out.reshape(n_exp, FF, k_out)
    flat = routes.reshape(-1)
    grad_flat = grads.reshape(tok * top, FF)
    bound = N_ROWS * N_EXPERT * CAP
    entries = jnp.arange(tok * top, dtype=jnp.int32)
    seq_range = jnp.arange(SEQS, dtype=jnp.int32)

    def one_expert(expert):
        member = (flat == expert).astype(jnp.int32)
        place = jnp.cumsum(member) - 1
        target = jnp.where(member == 1, place, bound).astype(jnp.int32)
        source = jnp.zeros((bound + 1,), jnp.int32).at[target].set(entries)[:bound]
        filled = jnp.zeros((bound + 1,), jnp.int32).at[target].set(1)[:bound]
        token_of = (source // top).astype(jnp.int32)
        keep = filled.astype(jnp.bfloat16)[:, None]
        a_rows = acts[token_of] * keep
        g_rows = grad_flat[source] * keep
        u_rows = jnp.dot(a_rows, pin_all[expert], preferred_element_type=jnp.float32)
        v_rows = jnp.dot(g_rows, pout_all[expert], preferred_element_type=jnp.float32)
        labels = jnp.where(filled == 1, seq_ids[token_of], -1)
        onehot = (labels[None, :] == seq_range[:, None]).astype(jnp.float32)
        outer = (u_rows[:, :, None] * v_rows[:, None, :]).reshape(bound, k_in * k_out)
        return jnp.dot(onehot, outer, precision=lax.Precision.HIGHEST)

    stacked = lax.map(one_expert, jnp.arange(n_exp, dtype=jnp.int32))
    return jnp.transpose(stacked, (1, 0, 2))
```

```python
import functools

import jax
import jax.numpy as jnp
from jax import lax
from jax.experimental import pallas as pl
from jax.experimental.pallas import tpu as pltpu
from jax.sharding import PartitionSpec as P

SEQS = 4
AXES = ("groups", "rows", "expert", "pair")
MESH = pl.DeviceIdType.MESH


def per_device(acts, grads, routes, seq_ids, p_in, p_out):
    tok, top = routes.shape
    half_d, half_ff = acts.shape[1], grads.shape[2]
    k_in, k_out = p_in.shape[3], p_out.shape[3]
    feat = k_in * k_out
    n_rows, n_exp = lax.axis_size("rows"), lax.axis_size("expert")
    capacity = min(tok, 3 * tok // n_exp)
    d_piece, f_piece = half_d // n_rows, half_ff // n_rows
    member = (routes.reshape(-1)[:, None] == jnp.arange(n_exp)[None, :]).astype(jnp.int32)
    before = jnp.tri(tok * top, k=-1, dtype=jnp.bfloat16)
    places = jnp.dot(
        before, member.astype(jnp.bfloat16), preferred_element_type=jnp.float32
    ).astype(jnp.int32)
    hits = (member[:, :, None] == 1) & (places[:, :, None] == jnp.arange(capacity)[None, None, :])
    hits = hits.reshape(tok * top, n_exp * capacity)
    pick = hits.T.astype(jnp.bfloat16)
    pick_tok = pick.reshape(-1, tok, top).sum(axis=2)
    a_b = jnp.dot(pick_tok, acts, preferred_element_type=jnp.float32).astype(jnp.bfloat16)
    g_b = jnp.dot(
        pick, grads.reshape(tok * top, half_ff), preferred_element_type=jnp.float32
    ).astype(jnp.bfloat16)
    entry_seq = jnp.broadcast_to(seq_ids[:, None], (tok, top)).reshape(-1)
    labels = jnp.sum(jnp.where(hits, entry_seq[:, None] + 1, 0), axis=0) - 1
    labels = labels.astype(jnp.bfloat16).reshape(1, n_exp, capacity)

    def swap(block):
        return lax.all_to_all(
            block.reshape((n_rows * n_exp,) + block.shape[2:]), ("rows", "expert"),
            split_axis=0, concat_axis=0, tiled=True,
        )

    a_rows = swap(a_b.reshape(n_exp, capacity, n_rows, d_piece).transpose(2, 0, 1, 3))
    g_rows = swap(g_b.reshape(n_exp, capacity, n_rows, f_piece).transpose(2, 0, 1, 3))
    label_rows = swap(jnp.broadcast_to(labels, (n_rows, n_exp, capacity)))
    slots = n_rows * n_exp * capacity
    slot_labels = label_rows.reshape(slots).astype(jnp.int32)
    u_part = jnp.dot(
        a_rows.reshape(slots, d_piece), p_in.reshape(d_piece, k_in),
        preferred_element_type=jnp.float32,
    )
    v_part = jnp.dot(
        g_rows.reshape(slots, f_piece), p_out.reshape(f_piece, k_out),
        preferred_element_type=jnp.float32,
    )
    u_all, v_all = lax.psum((u_part, v_part), ("rows", "pair"))
    cols = k_in // lax.axis_size(("rows", "pair"))
    u_cols = lax.dynamic_slice_in_dim(
        u_all, lax.axis_index(("rows", "pair")) * cols, cols, axis=1
    )
    onehot = (slot_labels[:, None] == jnp.arange(SEQS)[None, :]).astype(jnp.float32)
    left = (onehot[:, :, None] * u_cols[:, None, :]).reshape(slots, SEQS * cols)
    block = lax.dot_general(
        left, v_all, (((0,), (0,)), ((), ())), precision=lax.Precision.HIGHEST
    )
    return block.reshape(SEQS, 1, cols * k_out)


def exchange_kernel(
    sizes, acts, grads, routes, seq, p_in, p_out, out,
    a_buf, g_buf, r_buf, wi_buf, wo_buf, cnt_buf, p_buf, s1_buf, e_buf, s2_buf, t_buf, f_buf,
    loc_sem, a_ss, a_rs, g_ss, g_rs, r_ss, r_rs, wi_ss, wi_rs, wo_ss, wo_rs, c_ss, c_rs,
    s1_ss, s1_rs, s2_ss, s2_rs,
):
    n_g, n_r, n_e, n_h = sizes
    n_q = n_g * n_r
    n_slab = n_q * n_h
    n_chip = n_r * n_e
    g, x, z, h = (lax.axis_index(name) for name in AXES)
    q = g * n_r + x
    me = q * n_h + h
    chip = x * n_e + z
    tok, da = a_buf.shape[1], a_buf.shape[2]
    ent, df = g_buf.shape[1], g_buf.shape[2]
    top = ent // tok
    part = tok // n_h

    def rcopy(src, dst, ss, rs, dev):
        return pltpu.make_async_remote_copy(
            src_ref=src, dst_ref=dst, send_sem=ss, recv_sem=rs,
            device_id=dev, device_id_type=MESH,
        )

    def span(gg, xx, width):
        return pl.ds(pl.multiple_of((xx * n_g + gg) * width, 128), width)

    slab = []
    for j in range(1, n_q):
        o = lax.rem(q + j, n_q)
        slab.append((o, o // n_r, lax.rem(o, n_r)))

    wcol_i = pl.ds(pl.multiple_of(g * da, 128), da)
    wcol_o = pl.ds(pl.multiple_of(g * df, 128), df)
    local = [
        pltpu.make_async_copy(acts.at[:, span(g, x, da)], a_buf.at[q], loc_sem.at[0]),
        pltpu.make_async_copy(grads.at[:, span(g, x, df)], g_buf.at[q], loc_sem.at[1]),
        pltpu.make_async_copy(p_in.at[:, wcol_i], wi_buf.at[z], loc_sem.at[2]),
        pltpu.make_async_copy(p_out.at[:, wcol_o], wo_buf.at[z], loc_sem.at[3]),
    ]
    for c in local:
        c.start()

    barrier = pltpu.get_barrier_semaphore()
    count = 0
    for j in range(1, n_slab):
        o = lax.rem(me + j, n_slab)
        oq = o // n_h
        pl.semaphore_signal(
            barrier, inc=1, device_id=(oq // n_r, lax.rem(oq, n_r), z, lax.rem(o, n_h)),
            device_id_type=MESH,
        )
        count += 1
    for j in range(1, n_e):
        oz = lax.rem(z + j, n_e)
        for ox in range(n_r):
            for oh in range(n_h):
                pl.semaphore_signal(barrier, inc=1, device_id=(g, ox, oz, oh), device_id_type=MESH)
                count += 1

    eye = lax.broadcasted_iota(jnp.int32, (tok, tok), 0) == lax.broadcasted_iota(
        jnp.int32, (tok, tok), 1
    )
    for k in range(top):
        row = routes[k : k + 1, :].astype(jnp.float32)
        col = jnp.sum(jnp.where(eye, jnp.broadcast_to(row, (tok, tok)), 0.0), axis=1, keepdims=True)
        r_buf[q, k] = jnp.broadcast_to(col, (tok, 128)).astype(jnp.bfloat16)
    upto = (
        jnp.broadcast_to(seq[...], (8, tok)) <= lax.broadcasted_iota(jnp.int32, (8, tok), 0)
    ).astype(jnp.float32)
    cnt_buf[chip] = jnp.broadcast_to(jnp.sum(upto, axis=1, keepdims=True), (8, 128))

    pl.semaphore_wait(barrier, count)

    def wi_copy(src, owner, to, d):
        return rcopy(src, wi_buf.at[owner], wi_ss.at[d, owner], wi_rs.at[owner], (g, x, to, h))

    def wo_copy(src, owner, to, d):
        return rcopy(src, wo_buf.at[owner], wo_ss.at[d, owner], wo_rs.at[owner], (g, x, to, h))

    for d, step, ok in ((0, 1, z < n_e - 1), (1, -1, z > 0)):

        @pl.when(ok)
        def _():
            wi_copy(p_in.at[:, wcol_i], z, z + step, d).start()
            wo_copy(p_out.at[:, wcol_o], z, z + step, d).start()

    sends = []
    for j, (o, og, ox) in enumerate(slab):
        dev = (og, ox, z, h)
        sends.append(rcopy(r_buf.at[q], r_buf.at[q], r_ss.at[j], r_rs.at[q], dev))
        sends.append(rcopy(acts.at[:, span(og, ox, da)], a_buf.at[q], a_ss.at[j], a_rs.at[q], dev))
        sends.append(rcopy(grads.at[:, span(og, ox, df)], g_buf.at[q], g_ss.at[j], g_rs.at[q], dev))
    others = []
    for j in range(1, n_chip):
        o = lax.rem(chip + j, n_chip)
        others.append(o)
        dev = (g, o // n_e, lax.rem(o, n_e), h)
        sends.append(
            rcopy(cnt_buf.at[chip], cnt_buf.at[chip], c_ss.at[j - 1], c_rs.at[chip], dev)
        )
    for c in sends:
        c.start()

    for step in range(1, n_e):
        for d, sign in ((0, 1), (1, -1)):
            owner = z - sign * step

            @pl.when((owner >= 0) & (owner < n_e))
            def _():
                to = z + sign
                inside = (to >= 0) & (to < n_e)
                wi_copy(wi_buf.at[owner], owner, z, d).wait_recv()

                @pl.when(inside)
                def _():
                    wi_copy(wi_buf.at[owner], owner, to, d).start()

                wo_copy(wo_buf.at[owner], owner, z, d).wait_recv()

                @pl.when(inside)
                def _():
                    wo_copy(wo_buf.at[owner], owner, to, d).start()

    for c in local:
        c.wait()
    here = (g, x, z, h)
    for o, og, ox in slab:
        rcopy(r_buf.at[o], r_buf.at[o], r_ss.at[0], r_rs.at[o], here).wait_recv()
        rcopy(a_buf.at[o], a_buf.at[o], a_ss.at[0], a_rs.at[o], here).wait_recv()
        rcopy(g_buf.at[o], g_buf.at[o], g_ss.at[0], g_rs.at[o], here).wait_recv()

    k_in = wi_buf.shape[1]
    nt = (((1,), (1,)), ((), ()))
    u_all = lax.dot_general(
        a_buf[...].reshape(n_q * tok, da), wi_buf[...].reshape(n_e * k_in, da), nt,
        preferred_element_type=jnp.float32,
    )
    v_all = lax.dot_general(
        g_buf[...].reshape(n_q * ent, df), wo_buf[...].reshape(n_e * k_in, df), nt,
        preferred_element_type=jnp.float32,
    )
    lane = lax.broadcasted_iota(jnp.int32, (tok, 128), 1)
    left = lane < 64
    half_of = jnp.where(left, 0.0, 1.0)

    def picked(rows, ids):
        total = jnp.zeros((tok, 128), jnp.float32)
        for c in range(n_e // 2):
            total += jnp.where(ids == half_of + 2.0 * c, rows[:, c * 128 : (c + 1) * 128], 0.0)
        return total + pltpu.roll(total, 64, 1)

    for o in range(n_q):
        for k in range(top):
            ids = r_buf[o, k].astype(jnp.float32)
            u = picked(u_all[o * tok : (o + 1) * tok], ids)
            v = picked(v_all[o * ent + k * tok : o * ent + (k + 1) * tok], ids)
            both = jnp.where(left, u, v)
            for t in range(n_h):
                p_buf[o, t, k] = both[t * part : (t + 1) * part]

    firsts = []
    for j in range(1, n_slab):
        o = lax.rem(me + j, n_slab)
        oq = o // n_h
        oh = lax.rem(o, n_h)
        c = rcopy(
            p_buf.at[oq, oh], s1_buf.at[me], s1_ss.at[j - 1], s1_rs.at[me],
            (oq // n_r, lax.rem(oq, n_r), z, oh),
        )
        c.start()
        firsts.append((o, c))
    total = p_buf[q, h]
    for o, c in firsts:
        rcopy(s1_buf.at[o], s1_buf.at[o], s1_ss.at[0], s1_rs.at[o], here).wait_recv()
        total += s1_buf[o]
    mine = pl.ds(pl.multiple_of(h * part, 16), part)
    ids = [r_buf[q, k, mine].astype(jnp.float32) for k in range(top)]
    for e in range(n_e):
        m = jnp.zeros((part, 128), jnp.float32)
        for k in range(top):
            m += jnp.where(ids[k] == float(e), total[k], 0.0)
        e_buf[e] = m

    spot = chip * n_h + h
    s2_buf[spot] = e_buf[z]
    n_group = n_chip * n_h
    seconds = []
    for j in range(1, n_group):
        o = lax.rem(spot + j, n_group)
        oc = o // n_h
        oz = lax.rem(oc, n_e)
        c = rcopy(
            e_buf.at[oz], s2_buf.at[spot], s2_ss.at[j - 1], s2_rs.at[spot],
            (g, oc // n_e, oz, lax.rem(o, n_h)),
        )
        c.start()
        seconds.append((o, c))
    cum = cnt_buf[chip]
    for o in others:
        rcopy(cnt_buf.at[o], cnt_buf.at[o], c_ss.at[0], c_rs.at[o], here).wait_recv()
        cum += cnt_buf[o]
    for o, c in seconds:
        rcopy(s2_buf.at[o], s2_buf.at[o], s2_ss.at[0], s2_rs.at[o], here).wait_recv()
    rows = n_group * part
    uv = s2_buf[...].reshape(rows, 128)
    t_buf[...] = uv.T
    cols = k_in // (n_r * n_h)
    ut = t_buf[pl.ds(pl.multiple_of((x * n_h + h) * cols, 8), cols), :]
    pos = lax.broadcasted_iota(jnp.int32, (cols, rows), 1).astype(jnp.float32)
    blocks = []
    for s in range(SEQS):
        keep = pos < cum[s : s + 1, 0:1]
        if s:
            keep &= pos >= cum[s - 1 : s, 0:1]
        blocks.append(jnp.where(keep, ut, 0.0))
    f_buf[...] = lax.dot_general(
        jnp.concatenate(blocks, axis=0), uv, (((1,), (0,)), ((), ())),
        precision=lax.Precision.HIGHEST, preferred_element_type=jnp.float32,
    )
    n_out = SEQS * cols // 2
    even = f_buf[pl.ds(0, n_out, stride=2), :]
    odd = f_buf[pl.ds(1, n_out, stride=2), :]
    out[...] = jnp.where(
        lax.broadcasted_iota(jnp.int32, (n_out, 128), 1) < 64, pltpu.roll(even, 64, 1), odd
    )

    for d, sign in ((0, 1), (1, -1)):
        to = z + sign
        for step in range(n_e):
            owner = z - sign * step

            @pl.when((owner >= 0) & (owner < n_e) & (to >= 0) & (to < n_e))
            def _():
                wi_copy(wi_buf.at[owner], owner, to, d).wait_send()
                wo_copy(wo_buf.at[owner], owner, to, d).wait_send()

    for c in sends:
        c.wait_send()
    for _, c in firsts + seconds:
        c.wait_send()


def per_device_fused(sizes, acts, grads, routes, seq_ids, p_in, p_out):
    n_g, n_r, n_e, n_h = sizes
    tok, half_d = acts.shape
    top, half_ff = grads.shape[1], grads.shape[2]
    k_in = p_in.shape[3]
    n_q = n_g * n_r
    da, df = half_d // n_q, half_ff // n_q
    ent = tok * top
    n_slab, n_chip = n_q * n_h, n_r * n_e
    n_group = n_chip * n_h
    part = tok // n_h
    cols = k_in // (n_r * n_h)
    n_out = SEQS * cols // 2
    bf, f32, dma = jnp.bfloat16, jnp.float32, pltpu.SemaphoreType.DMA
    vmem = pl.BlockSpec(memory_space=pltpu.VMEM)
    hbm = pl.BlockSpec(memory_space=pl.ANY)
    features = pl.pallas_call(
        functools.partial(exchange_kernel, sizes),
        out_shape=jax.ShapeDtypeStruct((n_out, 128), f32),
        in_specs=[hbm, hbm, vmem, vmem, hbm, hbm],
        out_specs=vmem,
        scratch_shapes=[
            pltpu.VMEM((n_q, tok, da), bf),
            pltpu.VMEM((n_q, ent, df), bf),
            pltpu.VMEM((n_q, top, tok, 128), bf),
            pltpu.VMEM((n_e, k_in, da), bf),
            pltpu.VMEM((n_e, k_in, df), bf),
            pltpu.VMEM((n_chip, 8, 128), f32),
            pltpu.VMEM((n_q, n_h, top, part, 128), f32),
            pltpu.VMEM((n_slab, top, part, 128), f32),
            pltpu.VMEM((n_e, part, 128), f32),
            pltpu.VMEM((n_group, part, 128), f32),
            pltpu.VMEM((128, n_group * part), f32),
            pltpu.VMEM((SEQS * cols, 128), f32),
            dma((4,)),
            dma((n_q,)), dma((n_q,)), dma((n_q,)), dma((n_q,)), dma((n_q,)), dma((n_q,)),
            dma((2, n_e)), dma((n_e,)), dma((2, n_e)), dma((n_e,)),
            dma((n_chip,)), dma((n_chip,)),
            dma((n_slab,)), dma((n_slab,)),
            dma((n_group,)), dma((n_group,)),
        ],
        compiler_params=pltpu.CompilerParams(
            collective_id=0, has_side_effects=True, vmem_limit_bytes=24 * 1024 * 1024
        ),
    )(
        acts,
        grads.transpose(1, 0, 2).reshape(ent, half_ff),
        routes.T,
        seq_ids.reshape(1, tok),
        p_in.reshape(p_in.shape[2], k_in).T,
        p_out.reshape(p_out.shape[2], k_in).T,
    )
    return features.reshape(SEQS, 1, -1)


def fits(sizes):
    n_g, n_r, n_e, n_h = sizes
    return n_g * n_r <= 4 and n_e % 2 == 0 and n_e <= 4 and n_h == 2


def solution(mesh):
    sizes = tuple(mesh.shape[name] for name in AXES)
    body = functools.partial(per_device_fused, sizes) if fits(sizes) else per_device
    return jax.shard_map(
        body,
        mesh=mesh,
        in_specs=(
            P(("groups", "rows", "expert"), "pair"),
            P(("groups", "rows", "expert"), None, "pair"),
            P(("groups", "rows", "expert"), None),
            P(("groups", "rows", "expert")),
            P("expert", "pair", "rows", None),
            P("expert", "pair", "rows", None),
        ),
        out_specs=P("groups", "expert", ("rows", "pair")),
        check_vma=False,
    )
```

```python
import functools

import jax
import jax.numpy as jnp
from jax import lax
from jax.experimental import pallas as pl
from jax.experimental.pallas import tpu as pltpu
from jax.sharding import PartitionSpec as P

SEQS = 4
AXES = ("groups", "rows", "expert", "pair")
MESH = pl.DeviceIdType.MESH


def per_device(acts, grads, routes, seq_ids, p_in, p_out):
    tok, top = routes.shape
    half_d, half_ff = acts.shape[1], grads.shape[2]
    k_in, k_out = p_in.shape[3], p_out.shape[3]
    feat = k_in * k_out
    n_rows, n_exp = lax.axis_size("rows"), lax.axis_size("expert")
    capacity = min(tok, 3 * tok // n_exp)
    d_piece, f_piece = half_d // n_rows, half_ff // n_rows
    member = (routes.reshape(-1)[:, None] == jnp.arange(n_exp)[None, :]).astype(jnp.int32)
    before = jnp.tri(tok * top, k=-1, dtype=jnp.bfloat16)
    places = jnp.dot(
        before, member.astype(jnp.bfloat16), preferred_element_type=jnp.float32
    ).astype(jnp.int32)
    hits = (member[:, :, None] == 1) & (places[:, :, None] == jnp.arange(capacity)[None, None, :])
    hits = hits.reshape(tok * top, n_exp * capacity)
    pick = hits.T.astype(jnp.bfloat16)
    pick_tok = pick.reshape(-1, tok, top).sum(axis=2)
    a_b = jnp.dot(pick_tok, acts, preferred_element_type=jnp.float32).astype(jnp.bfloat16)
    g_b = jnp.dot(
        pick, grads.reshape(tok * top, half_ff), preferred_element_type=jnp.float32
    ).astype(jnp.bfloat16)
    entry_seq = jnp.broadcast_to(seq_ids[:, None], (tok, top)).reshape(-1)
    labels = jnp.sum(jnp.where(hits, entry_seq[:, None] + 1, 0), axis=0) - 1
    labels = labels.astype(jnp.bfloat16).reshape(1, n_exp, capacity)

    def swap(block):
        return lax.all_to_all(
            block.reshape((n_rows * n_exp,) + block.shape[2:]), ("rows", "expert"),
            split_axis=0, concat_axis=0, tiled=True,
        )

    a_rows = swap(a_b.reshape(n_exp, capacity, n_rows, d_piece).transpose(2, 0, 1, 3))
    g_rows = swap(g_b.reshape(n_exp, capacity, n_rows, f_piece).transpose(2, 0, 1, 3))
    label_rows = swap(jnp.broadcast_to(labels, (n_rows, n_exp, capacity)))
    slots = n_rows * n_exp * capacity
    slot_labels = label_rows.reshape(slots).astype(jnp.int32)
    u_part = jnp.dot(
        a_rows.reshape(slots, d_piece), p_in.reshape(d_piece, k_in),
        preferred_element_type=jnp.float32,
    )
    v_part = jnp.dot(
        g_rows.reshape(slots, f_piece), p_out.reshape(f_piece, k_out),
        preferred_element_type=jnp.float32,
    )
    u_all, v_all = lax.psum((u_part, v_part), ("rows", "pair"))
    cols = k_in // lax.axis_size(("rows", "pair"))
    u_cols = lax.dynamic_slice_in_dim(
        u_all, lax.axis_index(("rows", "pair")) * cols, cols, axis=1
    )
    onehot = (slot_labels[:, None] == jnp.arange(SEQS)[None, :]).astype(jnp.float32)
    left = (onehot[:, :, None] * u_cols[:, None, :]).reshape(slots, SEQS * cols)
    block = lax.dot_general(
        left, v_all, (((0,), (0,)), ((), ())), precision=lax.Precision.HIGHEST
    )
    return block.reshape(SEQS, 1, cols * k_out)


def exchange_kernel(
    sizes, acts, grads, routes_hbm, seq_hbm, p_in, p_out, out,
    a_buf, g_buf, r_buf, wi_buf, wo_buf, cnt_buf, p_buf, s1_buf, e_buf, s2_buf, t_buf, f_buf, v_buf, g2_buf, routes, seq,
    loc_sem, a_ss, a_rs, g_ss, g_rs, r_ss, r_rs, wi_ss, wi_rs, wo_ss, wo_rs, c_ss, c_rs,
    s1_ss, s1_rs, s2_ss, s2_rs,
):
    n_g, n_r, n_e, n_h = sizes
    n_q = n_g * n_r
    n_slab = n_q * n_h
    n_chip = n_r * n_e
    g, x, z, h = (lax.axis_index(name) for name in AXES)
    q = g * n_r + x
    me = q * n_h + h
    chip = x * n_e + z
    tok, da = a_buf.shape[1], a_buf.shape[2]
    top, df = g_buf.shape[2], g_buf.shape[3]
    ent = tok * top
    part = tok // n_h

    def rcopy(src, dst, ss, rs, dev):
        return pltpu.make_async_remote_copy(
            src_ref=src, dst_ref=dst, send_sem=ss, recv_sem=rs,
            device_id=dev, device_id_type=MESH,
        )

    def span(gg, xx, width):
        return pl.ds(pl.multiple_of((xx * n_g + gg) * width, 128), width)

    slab = []
    for j in range(1, n_q):
        o = lax.rem(q + j, n_q)
        slab.append((o, o // n_r, lax.rem(o, n_r)))

    wcol_i = pl.ds(pl.multiple_of(g * da, 128), da)
    wcol_o = pl.ds(pl.multiple_of(g * df, 128), df)
    local = [
        pltpu.make_async_copy(acts.at[:, span(g, x, da)], a_buf.at[q], loc_sem.at[0]),
        pltpu.make_async_copy(grads.at[:, :, span(g, x, df)], g_buf.at[q], loc_sem.at[1]),
        pltpu.make_async_copy(p_in.at[:, wcol_i], wi_buf.at[z], loc_sem.at[2]),
        pltpu.make_async_copy(p_out.at[:, wcol_o], wo_buf.at[z], loc_sem.at[3]),
    ]
    small = [
        pltpu.make_async_copy(routes_hbm, routes, loc_sem.at[4]),
        pltpu.make_async_copy(seq_hbm, seq, loc_sem.at[5]),
    ]
    for c in small + local:
        c.start()

    barrier = pltpu.get_barrier_semaphore()
    count = 0
    for j in range(1, n_slab):
        o = lax.rem(me + j, n_slab)
        oq = o // n_h
        pl.semaphore_signal(
            barrier, inc=1, device_id=(oq // n_r, lax.rem(oq, n_r), z, lax.rem(o, n_h)),
            device_id_type=MESH,
        )
        count += 1
    for j in range(1, n_e):
        oz = lax.rem(z + j, n_e)
        for ox in range(n_r):
            for oh in range(n_h):
                pl.semaphore_signal(barrier, inc=1, device_id=(g, ox, oz, oh), device_id_type=MESH)
                count += 1

    for c in small:
        c.wait()
    eye = lax.broadcasted_iota(jnp.int32, (tok, tok), 0) == lax.broadcasted_iota(
        jnp.int32, (tok, tok), 1
    )
    for k in range(top):
        row = routes[k : k + 1, :].astype(jnp.float32)
        col = jnp.sum(jnp.where(eye, jnp.broadcast_to(row, (tok, tok)), 0.0), axis=1, keepdims=True)
        r_buf[q, k] = jnp.broadcast_to(col, (tok, 128)).astype(jnp.bfloat16)
    upto = (
        jnp.broadcast_to(seq[...], (8, tok)) <= lax.broadcasted_iota(jnp.int32, (8, tok), 0)
    ).astype(jnp.float32)
    cnt_buf[chip] = jnp.broadcast_to(jnp.sum(upto, axis=1, keepdims=True), (8, 128))

    pl.semaphore_wait(barrier, count)

    def wi_copy(src, owner, to, d):
        return rcopy(src, wi_buf.at[owner], wi_ss.at[d, owner], wi_rs.at[owner], (g, x, to, h))

    def wo_copy(src, owner, to, d):
        return rcopy(src, wo_buf.at[owner], wo_ss.at[d, owner], wo_rs.at[owner], (g, x, to, h))

    for d, step, ok in ((0, 1, z < n_e - 1), (1, -1, z > 0)):

        @pl.when(ok)
        def _():
            wi_copy(p_in.at[:, wcol_i], z, z + step, d).start()
            wo_copy(p_out.at[:, wcol_o], z, z + step, d).start()

    sends = []
    for j, (o, og, ox) in enumerate(slab):
        dev = (og, ox, z, h)
        sends.append(rcopy(r_buf.at[q], r_buf.at[q], r_ss.at[j], r_rs.at[q], dev))
        sends.append(rcopy(acts.at[:, span(og, ox, da)], a_buf.at[q], a_ss.at[j], a_rs.at[q], dev))
        sends.append(rcopy(grads.at[:, :, span(og, ox, df)], g_buf.at[q], g_ss.at[j], g_rs.at[q], dev))
    others = []
    for j in range(1, n_chip):
        o = lax.rem(chip + j, n_chip)
        others.append(o)
        dev = (g, o // n_e, lax.rem(o, n_e), h)
        sends.append(
            rcopy(cnt_buf.at[chip], cnt_buf.at[chip], c_ss.at[j - 1], c_rs.at[chip], dev)
        )
    for c in sends:
        c.start()

    for step in range(1, n_e):
        for d, sign in ((0, 1), (1, -1)):
            owner = z - sign * step

            @pl.when((owner >= 0) & (owner < n_e))
            def _():
                to = z + sign
                inside = (to >= 0) & (to < n_e)
                wi_copy(wi_buf.at[owner], owner, z, d).wait_recv()

                @pl.when(inside)
                def _():
                    wi_copy(wi_buf.at[owner], owner, to, d).start()

                wo_copy(wo_buf.at[owner], owner, z, d).wait_recv()

                @pl.when(inside)
                def _():
                    wo_copy(wo_buf.at[owner], owner, to, d).start()

        if step == 1:
            for c in local:
                c.wait()
            here = (g, x, z, h)
            for o, og, ox in slab:
                rcopy(r_buf.at[o], r_buf.at[o], r_ss.at[0], r_rs.at[o], here).wait_recv()
                rcopy(a_buf.at[o], a_buf.at[o], a_ss.at[0], a_rs.at[o], here).wait_recv()
                rcopy(g_buf.at[o], g_buf.at[o], g_ss.at[0], g_rs.at[o], here).wait_recv()
            g2_buf[...] = g_buf[...].reshape(n_q * ent, df)

    k_in = wi_buf.shape[1]
    nt = (((1,), (1,)), ((), ()))
    u_all = lax.dot_general(
        a_buf[...].reshape(n_q * tok, da), wi_buf[...].reshape(n_e * k_in, da), nt,
        preferred_element_type=jnp.float32,
    )
    v_all = lax.dot_general(
        g2_buf[...], wo_buf[...].reshape(n_e * k_in, df), nt,
        preferred_element_type=jnp.float32,
    )
    for c in range(n_e // 2):
        v_buf[c] = v_all[:, c * 128 : (c + 1) * 128]
    lane = lax.broadcasted_iota(jnp.int32, (tok, 128), 1)
    left = lane < 64
    half_of = jnp.where(left, 0.0, 1.0)

    def picked(rows, ids):
        total = jnp.zeros((tok, 128), jnp.float32)
        for c in range(n_e // 2):
            total += jnp.where(ids == half_of + 2.0 * c, rows[c], 0.0)
        return total + pltpu.roll(total, 64, 1)

    for o in range(n_q):
        for k in range(top):
            ids = r_buf[o, k].astype(jnp.float32)
            u = picked([u_all[o * tok : (o + 1) * tok, c * 128 : (c + 1) * 128] for c in range(n_e // 2)], ids)
            v = picked([v_buf[c, pl.ds(o * ent + k, tok, stride=top), :] for c in range(n_e // 2)], ids)
            both = jnp.where(left, u, v)
            for t in range(n_h):
                p_buf[o, t, k] = both[t * part : (t + 1) * part]

    firsts = []
    for j in range(1, n_slab):
        o = lax.rem(me + j, n_slab)
        oq = o // n_h
        oh = lax.rem(o, n_h)
        c = rcopy(
            p_buf.at[oq, oh], s1_buf.at[me], s1_ss.at[j - 1], s1_rs.at[me],
            (oq // n_r, lax.rem(oq, n_r), z, oh),
        )
        c.start()
        firsts.append((o, c))
    total = p_buf[q, h]
    for o, c in firsts:
        rcopy(s1_buf.at[o], s1_buf.at[o], s1_ss.at[0], s1_rs.at[o], here).wait_recv()
        total += s1_buf[o]
    mine = pl.ds(pl.multiple_of(h * part, 16), part)
    ids = [r_buf[q, k, mine].astype(jnp.float32) for k in range(top)]
    for e in range(n_e):
        m = jnp.zeros((part, 128), jnp.float32)
        for k in range(top):
            m += jnp.where(ids[k] == float(e), total[k], 0.0)
        e_buf[e] = m

    spot = chip * n_h + h
    s2_buf[spot] = e_buf[z]
    n_group = n_chip * n_h
    seconds = []
    for j in range(1, n_group):
        o = lax.rem(spot + j, n_group)
        oc = o // n_h
        oz = lax.rem(oc, n_e)
        c = rcopy(
            e_buf.at[oz], s2_buf.at[spot], s2_ss.at[j - 1], s2_rs.at[spot],
            (g, oc // n_e, oz, lax.rem(o, n_h)),
        )
        c.start()
        seconds.append((o, c))
    cum = cnt_buf[chip]
    for o in others:
        rcopy(cnt_buf.at[o], cnt_buf.at[o], c_ss.at[0], c_rs.at[o], here).wait_recv()
        cum += cnt_buf[o]
    for o, c in seconds:
        rcopy(s2_buf.at[o], s2_buf.at[o], s2_ss.at[0], s2_rs.at[o], here).wait_recv()
    rows = n_group * part
    uv = s2_buf[...].reshape(rows, 128)
    t_buf[...] = uv.T
    cols = k_in // (n_r * n_h)
    ut = t_buf[pl.ds(pl.multiple_of((x * n_h + h) * cols, 8), cols), :]
    pos = lax.broadcasted_iota(jnp.int32, (cols, rows), 1).astype(jnp.float32)
    blocks = []
    for s in range(SEQS):
        keep = pos < cum[s : s + 1, 0:1]
        if s:
            keep &= pos >= cum[s - 1 : s, 0:1]
        blocks.append(jnp.where(keep, ut, 0.0))
    f_buf[...] = lax.dot_general(
        jnp.concatenate(blocks, axis=0), uv, (((1,), (0,)), ((), ())),
        precision=lax.Precision.HIGHEST, preferred_element_type=jnp.float32,
    )
    n_out = SEQS * cols // 2
    even = f_buf[pl.ds(0, n_out, stride=2), :]
    odd = f_buf[pl.ds(1, n_out, stride=2), :]
    out[...] = jnp.where(
        lax.broadcasted_iota(jnp.int32, (n_out, 128), 1) < 64, pltpu.roll(even, 64, 1), odd
    )

    for d, sign in ((0, 1), (1, -1)):
        to = z + sign
        for step in range(n_e):
            owner = z - sign * step

            @pl.when((owner >= 0) & (owner < n_e) & (to >= 0) & (to < n_e))
            def _():
                wi_copy(wi_buf.at[owner], owner, to, d).wait_send()
                wo_copy(wo_buf.at[owner], owner, to, d).wait_send()

    for c in sends:
        c.wait_send()
    for _, c in firsts + seconds:
        c.wait_send()


def per_device_fused(sizes, acts, grads, routes, seq_ids, p_in, p_out):
    n_g, n_r, n_e, n_h = sizes
    tok, half_d = acts.shape
    top, half_ff = grads.shape[1], grads.shape[2]
    k_in = p_in.shape[3]
    n_q = n_g * n_r
    da, df = half_d // n_q, half_ff // n_q
    ent = tok * top
    n_slab, n_chip = n_q * n_h, n_r * n_e
    n_group = n_chip * n_h
    part = tok // n_h
    cols = k_in // (n_r * n_h)
    n_out = SEQS * cols // 2
    bf, f32, dma = jnp.bfloat16, jnp.float32, pltpu.SemaphoreType.DMA
    vmem = pl.BlockSpec(memory_space=pltpu.VMEM)
    hbm = pl.BlockSpec(memory_space=pltpu.HBM)
    features = pl.pallas_call(
        functools.partial(exchange_kernel, sizes),
        out_shape=jax.ShapeDtypeStruct((n_out, 128), f32),
        in_specs=[hbm] * 6,
        out_specs=vmem,
        scratch_shapes=[
            pltpu.VMEM((n_q, tok, da), bf),
            pltpu.VMEM((n_q, tok, top, df), bf),
            pltpu.VMEM((n_q, top, tok, 128), bf),
            pltpu.VMEM((n_e, k_in, da), bf),
            pltpu.VMEM((n_e, k_in, df), bf),
            pltpu.VMEM((n_chip, 8, 128), f32),
            pltpu.VMEM((n_q, n_h, top, part, 128), f32),
            pltpu.VMEM((n_slab, top, part, 128), f32),
            pltpu.VMEM((n_e, part, 128), f32),
            pltpu.VMEM((n_group, part, 128), f32),
            pltpu.VMEM((128, n_group * part), f32),
            pltpu.VMEM((SEQS * cols, 128), f32),
            pltpu.VMEM((n_e // 2, n_q * ent, 128), f32),
            pltpu.VMEM((n_q * ent, df), bf),
            pltpu.VMEM((top, tok), jnp.int32),
            pltpu.VMEM((1, tok), jnp.int32),
            dma((6,)),
            dma((n_q,)), dma((n_q,)), dma((n_q,)), dma((n_q,)), dma((n_q,)), dma((n_q,)),
            dma((2, n_e)), dma((n_e,)), dma((2, n_e)), dma((n_e,)),
            dma((n_chip,)), dma((n_chip,)),
            dma((n_slab,)), dma((n_slab,)),
            dma((n_group,)), dma((n_group,)),
        ],
        compiler_params=pltpu.CompilerParams(
            collective_id=0, has_side_effects=True, vmem_limit_bytes=60 * 1024 * 1024
        ),
    )(
        acts,
        grads,
        routes.T,
        seq_ids.reshape(1, tok),
        p_in.reshape(p_in.shape[2], k_in).T,
        p_out.reshape(p_out.shape[2], k_in).T,
    )
    return features.reshape(SEQS, 1, -1)


def fits(sizes):
    n_g, n_r, n_e, n_h = sizes
    return n_g * n_r <= 4 and n_e % 2 == 0 and n_e <= 4 and n_h == 2


def solution(mesh):
    sizes = tuple(mesh.shape[name] for name in AXES)
    body = functools.partial(per_device_fused, sizes) if fits(sizes) else per_device
    return jax.shard_map(
        body,
        mesh=mesh,
        in_specs=(
            P(("groups", "rows", "expert"), "pair"),
            P(("groups", "rows", "expert"), None, "pair"),
            P(("groups", "rows", "expert"), None),
            P(("groups", "rows", "expert")),
            P("expert", "pair", "rows", None),
            P("expert", "pair", "rows", None),
        ),
        out_specs=P("groups", "expert", ("rows", "pair")),
        check_vma=False,
    )
```

```python
import functools

import jax
import jax.numpy as jnp
from jax import lax
from jax.experimental import pallas as pl
from jax.experimental.pallas import tpu as pltpu
from jax.sharding import PartitionSpec as P

SEQS = 4
AXES = ("groups", "rows", "expert", "pair")
MESH = pl.DeviceIdType.MESH


def per_device(acts, grads, routes, seq_ids, p_in, p_out):
    tok, top = routes.shape
    half_d, half_ff = acts.shape[1], grads.shape[2]
    k_in, k_out = p_in.shape[3], p_out.shape[3]
    feat = k_in * k_out
    n_rows, n_exp = lax.axis_size("rows"), lax.axis_size("expert")
    capacity = min(tok, 3 * tok // n_exp)
    d_piece, f_piece = half_d // n_rows, half_ff // n_rows
    member = (routes.reshape(-1)[:, None] == jnp.arange(n_exp)[None, :]).astype(jnp.int32)
    before = jnp.tri(tok * top, k=-1, dtype=jnp.bfloat16)
    places = jnp.dot(
        before, member.astype(jnp.bfloat16), preferred_element_type=jnp.float32
    ).astype(jnp.int32)
    hits = (member[:, :, None] == 1) & (places[:, :, None] == jnp.arange(capacity)[None, None, :])
    hits = hits.reshape(tok * top, n_exp * capacity)
    pick = hits.T.astype(jnp.bfloat16)
    pick_tok = pick.reshape(-1, tok, top).sum(axis=2)
    a_b = jnp.dot(pick_tok, acts, preferred_element_type=jnp.float32).astype(jnp.bfloat16)
    g_b = jnp.dot(
        pick, grads.reshape(tok * top, half_ff), preferred_element_type=jnp.float32
    ).astype(jnp.bfloat16)
    entry_seq = jnp.broadcast_to(seq_ids[:, None], (tok, top)).reshape(-1)
    labels = jnp.sum(jnp.where(hits, entry_seq[:, None] + 1, 0), axis=0) - 1
    labels = labels.astype(jnp.bfloat16).reshape(1, n_exp, capacity)

    def swap(block):
        return lax.all_to_all(
            block.reshape((n_rows * n_exp,) + block.shape[2:]), ("rows", "expert"),
            split_axis=0, concat_axis=0, tiled=True,
        )

    a_rows = swap(a_b.reshape(n_exp, capacity, n_rows, d_piece).transpose(2, 0, 1, 3))
    g_rows = swap(g_b.reshape(n_exp, capacity, n_rows, f_piece).transpose(2, 0, 1, 3))
    label_rows = swap(jnp.broadcast_to(labels, (n_rows, n_exp, capacity)))
    slots = n_rows * n_exp * capacity
    slot_labels = label_rows.reshape(slots).astype(jnp.int32)
    u_part = jnp.dot(
        a_rows.reshape(slots, d_piece), p_in.reshape(d_piece, k_in),
        preferred_element_type=jnp.float32,
    )
    v_part = jnp.dot(
        g_rows.reshape(slots, f_piece), p_out.reshape(f_piece, k_out),
        preferred_element_type=jnp.float32,
    )
    u_all, v_all = lax.psum((u_part, v_part), ("rows", "pair"))
    cols = k_in // lax.axis_size(("rows", "pair"))
    u_cols = lax.dynamic_slice_in_dim(
        u_all, lax.axis_index(("rows", "pair")) * cols, cols, axis=1
    )
    onehot = (slot_labels[:, None] == jnp.arange(SEQS)[None, :]).astype(jnp.float32)
    left = (onehot[:, :, None] * u_cols[:, None, :]).reshape(slots, SEQS * cols)
    block = lax.dot_general(
        left, v_all, (((0,), (0,)), ((), ())), precision=lax.Precision.HIGHEST
    )
    return block.reshape(SEQS, 1, cols * k_out)


def exchange_kernel(
    sizes, acts, grads, routes_hbm, seq_hbm, p_in, p_out, out,
    a_buf, g_buf, r_buf, wi_buf, wo_buf, cnt_buf, p_buf, s1_buf, e_buf, s2_buf, t_buf, f_buf, v_buf, g2_buf, routes, seq,
    xa_buf, xg_buf, xr_buf, x_buf, u_buf,
    loc_sem, a_ss, a_rs, g_ss, g_rs, r_ss, r_rs, w_ss, w_rs, c_ss, c_rs,
    ae_ss, ae_rs, ge_ss, ge_rs, xa_ss, xa_rs, xg_ss, xg_rs, xr_ss, xr_rs, x_ss,
    s1_ss, s1_rs, s2_ss, s2_rs,
):
    n_g, n_r, n_e, n_h = sizes
    n_q = n_g * n_r
    n_slab = n_q * n_h
    n_chip = n_r * n_e
    g, x, z, h = (lax.axis_index(name) for name in AXES)
    q = g * n_r + x
    me = q * n_h + h
    chip = x * n_e + z
    tok, da = a_buf.shape[1], a_buf.shape[2]
    top, df = g_buf.shape[2], g_buf.shape[3]
    ent = tok * top
    part = tok // n_h

    def rcopy(src, dst, ss, rs, dev):
        return pltpu.make_async_remote_copy(
            src_ref=src, dst_ref=dst, send_sem=ss, recv_sem=rs,
            device_id=dev, device_id_type=MESH,
        )

    def span(gg, xx, width, first=0, size=None):
        start = pl.multiple_of((xx * n_g + gg) * width + first, 128)
        return pl.ds(start, width if size is None else size)

    ai, gi = xa_buf.shape[2], xg_buf.shape[3]
    a_main, g_main = pl.ds(ai, da - ai), pl.ds(gi, df - gi)
    a_lead, g_lead = pl.ds(0, ai), pl.ds(0, gi)
    at_end = (z == 0) | (z == n_e - 1)
    low = z * 2 < n_e
    ally = jnp.where(at_end, jnp.where(low, 1, n_e - 2), jnp.where(low, 0, n_e - 1))

    slab = []
    for j in range(1, n_q):
        o = lax.rem(q + j, n_q)
        slab.append((o, o // n_r, lax.rem(o, n_r)))

    wcol_i = pl.ds(pl.multiple_of(g * da, 128), da)
    wcol_o = pl.ds(pl.multiple_of(g * df, 128), df)
    local = [
        pltpu.make_async_copy(acts.at[:, span(g, x, da)], a_buf.at[q], loc_sem.at[0]),
        pltpu.make_async_copy(grads.at[:, :, span(g, x, df)], g_buf.at[q], loc_sem.at[1]),
        pltpu.make_async_copy(p_in.at[:, wcol_i], wi_buf.at[z], loc_sem.at[2]),
        pltpu.make_async_copy(p_out.at[:, wcol_o], wo_buf.at[z], loc_sem.at[3]),
    ]
    small = [
        pltpu.make_async_copy(routes_hbm, routes, loc_sem.at[4]),
        pltpu.make_async_copy(seq_hbm, seq, loc_sem.at[5]),
    ]
    for c in small + local:
        c.start()

    barrier = pltpu.get_barrier_semaphore()
    count = 0
    for j in range(1, n_slab):
        o = lax.rem(me + j, n_slab)
        oq = o // n_h
        pl.semaphore_signal(
            barrier, inc=1, device_id=(oq // n_r, lax.rem(oq, n_r), z, lax.rem(o, n_h)),
            device_id_type=MESH,
        )
        count += 1
    for j in range(1, n_e):
        oz = lax.rem(z + j, n_e)
        for ox in range(n_r):
            for oh in range(n_h):
                pl.semaphore_signal(barrier, inc=1, device_id=(g, ox, oz, oh), device_id_type=MESH)
                count += 1

    for j in range(1, n_g):
        for ox in range(n_r):
            for oh in range(n_h):
                pl.semaphore_signal(
                    barrier, inc=1, device_id=(lax.rem(g + j, n_g), ox, ally, oh),
                    device_id_type=MESH,
                )
                count += 1

    for c in small:
        c.wait()
    eye = lax.broadcasted_iota(jnp.int32, (tok, tok), 0) == lax.broadcasted_iota(
        jnp.int32, (tok, tok), 1
    )
    for k in range(top):
        row = routes[k : k + 1, :].astype(jnp.float32)
        col = jnp.sum(jnp.where(eye, jnp.broadcast_to(row, (tok, tok)), 0.0), axis=1, keepdims=True)
        r_buf[q, k] = jnp.broadcast_to(col, (tok, 128)).astype(jnp.bfloat16)
    upto = (
        jnp.broadcast_to(seq[...], (8, tok)) <= lax.broadcasted_iota(jnp.int32, (8, tok), 0)
    ).astype(jnp.float32)
    cnt_buf[chip] = jnp.broadcast_to(jnp.sum(upto, axis=1, keepdims=True), (8, 128))

    pl.semaphore_wait(barrier, count)

    kinds = (
        (p_in, wi_buf, g * da, a_lead, ai), (p_out, wo_buf, g * df, g_lead, gi),
        (p_in, wi_buf, g * da, a_main, da - ai), (p_out, wo_buf, g * df, g_main, df - gi),
    )

    def w_copy(kind, owner, to, d, own=False):
        hbm, buf, first, cols, size = kinds[kind]
        dst = buf.at[owner, :, cols]
        src = dst
        if own:
            src = hbm.at[:, pl.ds(pl.multiple_of(first + cols.start, 128), size)]
        return rcopy(src, dst, w_ss.at[kind, d, owner], w_rs.at[kind, owner], (g, x, to, h))

    def takes(kind, to):
        if kind < 2:
            return (to > 0) & (to < n_e - 1)
        return (to >= 0) & (to < n_e)

    ends, inners = [], []
    for j in range(n_q):
        o = lax.rem(q + j, n_q)
        og, ox = o // n_r, lax.rem(o, n_r)
        dev = (og, ox, ally, h)
        a_src, g_src = acts.at[:, span(og, ox, da, 0, ai)], grads.at[:, :, span(og, ox, df, 0, gi)]
        ends.append(rcopy(r_buf.at[q], xr_buf.at[q], xr_ss.at[j], xr_rs.at[q], dev))
        ends.append(rcopy(a_src, xa_buf.at[q], xa_ss.at[j], xa_rs.at[q], dev))
        ends.append(rcopy(g_src, xg_buf.at[q], xg_ss.at[j], xg_rs.at[q], dev))
        if j:
            dev = (og, ox, z, h)
            inners.append(
                rcopy(a_src, a_buf.at[q, :, a_lead], ae_ss.at[j], ae_rs.at[q], dev)
            )
            inners.append(
                rcopy(g_src, g_buf.at[q, :, :, g_lead], ge_ss.at[j], ge_rs.at[q], dev)
            )

    for kind in range(4):
        for d, step in ((0, 1), (1, -1)):

            @pl.when(takes(kind, z + step))
            def _():
                w_copy(kind, z, z + step, d, own=True).start()

    @pl.when(at_end)
    def _():
        for c in ends:
            c.start()

    @pl.when(jnp.logical_not(at_end))
    def _():
        for c in inners:
            c.start()

    sends = []
    for j, (o, og, ox) in enumerate(slab):
        dev = (og, ox, z, h)
        sends.append(rcopy(r_buf.at[q], r_buf.at[q], r_ss.at[j], r_rs.at[q], dev))
        sends.append(rcopy(acts.at[:, span(og, ox, da, ai, da - ai)], a_buf.at[q, :, a_main], a_ss.at[j], a_rs.at[q], dev))
        sends.append(rcopy(grads.at[:, :, span(og, ox, df, gi, df - gi)], g_buf.at[q, :, :, g_main], g_ss.at[j], g_rs.at[q], dev))
    others = []
    for j in range(1, n_chip):
        o = lax.rem(chip + j, n_chip)
        others.append(o)
        dev = (g, o // n_e, lax.rem(o, n_e), h)
        sends.append(
            rcopy(cnt_buf.at[chip], cnt_buf.at[chip], c_ss.at[j - 1], c_rs.at[chip], dev)
        )
    for c in sends:
        c.start()

    here = (g, x, z, h)

    def pass_on(step, kind_pair):
        for d, sign in ((0, 1), (1, -1)):
            owner = z - sign * step
            for kind in kind_pair:

                @pl.when((owner >= 0) & (owner < n_e) & takes(kind, z))
                def _():
                    w_copy(kind, owner, z, d).wait_recv()

                    @pl.when(takes(kind, z + sign))
                    def _():
                        w_copy(kind, owner, z + sign, d).start()

    k_in = wi_buf.shape[1]
    nt = (((1,), (1,)), ((), ()))
    left = lax.broadcasted_iota(jnp.int32, (tok, 128), 1) < 64
    half_of = jnp.where(left, 0.0, 1.0)

    def picked(rows, ids):
        total = jnp.zeros((tok, 128), jnp.float32)
        for c in range(n_e // 2):
            total += jnp.where(ids == half_of + 2.0 * c, rows[c], 0.0)
        return total + pltpu.roll(total, 64, 1)

    def project(a_rows, g_rows, w_a, w_g):
        u = lax.dot_general(
            a_rows.reshape(n_q * tok, -1), w_a.reshape(n_e * k_in, -1), nt,
            preferred_element_type=jnp.float32,
        )
        v = lax.dot_general(
            g_rows, w_g.reshape(n_e * k_in, -1), nt, preferred_element_type=jnp.float32
        )
        for c in range(n_e // 2):
            u_buf[c] = u[:, c * 128 : (c + 1) * 128]
            v_buf[c] = v[:, c * 128 : (c + 1) * 128]

    def choose(ids_ref, dst):
        for o in range(n_q):
            for k in range(top):
                ids = ids_ref[o, k].astype(jnp.float32)
                u = picked([u_buf[c, o * tok : (o + 1) * tok, :] for c in range(n_e // 2)], ids)
                v = picked(
                    [
                        v_buf[c, pl.ds(o * ent + k, tok, stride=top), :]
                        for c in range(n_e // 2)
                    ],
                    ids,
                )
                both = jnp.where(left, u, v)
                for t in range(n_h):
                    dst[o, t, k] = both[t * part : (t + 1) * part]

    pass_on(1, (0, 1, 2, 3))
    pass_on(2, (0, 1, 2, 3))
    for c in local:
        c.wait()
    for o, og, ox in slab:
        rcopy(r_buf.at[o], r_buf.at[o], r_ss.at[0], r_rs.at[o], here).wait_recv()
        rows = a_buf.at[o, :, a_main]
        rcopy(rows, rows, a_ss.at[0], a_rs.at[o], here).wait_recv()
        rows = g_buf.at[o, :, :, g_main]
        rcopy(rows, rows, g_ss.at[0], g_rs.at[o], here).wait_recv()

    extras = []
    for j in range(n_slab):
        o = lax.rem(me + j, n_slab)
        oq, oh = o // n_h, lax.rem(o, n_h)
        extras.append(
            rcopy(
                x_buf.at[oq, oh], s1_buf.at[n_slab + me], x_ss.at[j], s1_rs.at[n_slab + me],
                (oq // n_r, lax.rem(oq, n_r), ally, oh),
            )
        )

    @pl.when(jnp.logical_not(at_end))
    def _():
        for o in range(n_q):
            rcopy(xr_buf.at[o], xr_buf.at[o], xr_ss.at[0], xr_rs.at[o], here).wait_recv()
            rcopy(xa_buf.at[o], xa_buf.at[o], xa_ss.at[0], xa_rs.at[o], here).wait_recv()
            rcopy(xg_buf.at[o], xg_buf.at[o], xg_ss.at[0], xg_rs.at[o], here).wait_recv()
        project(
            xa_buf[...], xg_buf[...].reshape(n_q * ent, gi), wi_buf[:, :, :ai], wo_buf[:, :, :gi]
        )
        choose(xr_buf, x_buf)
        for c in extras:
            c.start()
        for o, og, ox in slab:
            rows = a_buf.at[o, :, a_lead]
            rcopy(rows, rows, ae_ss.at[0], ae_rs.at[o], here).wait_recv()
            rows = g_buf.at[o, :, :, g_lead]
            rcopy(rows, rows, ge_ss.at[0], ge_rs.at[o], here).wait_recv()
        g2_buf[...] = g_buf[...].reshape(n_q * ent, df)
        project(a_buf[...], g2_buf[...], wi_buf[...], wo_buf[...])

    @pl.when(at_end)
    def _():
        g2_buf[:, gi:] = g_buf[:, :, :, gi:].reshape(n_q * ent, df - gi)

    for step in range(3, n_e):
        pass_on(step, (2, 3))

    @pl.when(at_end)
    def _():
        project(a_buf[:, :, ai:], g2_buf[:, gi:], wi_buf[:, :, ai:], wo_buf[:, :, gi:])

    choose(r_buf, p_buf)

    firsts = []
    for j in range(1, n_slab):
        o = lax.rem(me + j, n_slab)
        oq = o // n_h
        oh = lax.rem(o, n_h)
        c = rcopy(
            p_buf.at[oq, oh], s1_buf.at[me], s1_ss.at[j - 1], s1_rs.at[me],
            (oq // n_r, lax.rem(oq, n_r), z, oh),
        )
        c.start()
        firsts.append((o, c))
    total = p_buf[q, h]
    for o, c in firsts:
        rcopy(s1_buf.at[o], s1_buf.at[o], s1_ss.at[0], s1_rs.at[o], here).wait_recv()
        total += s1_buf[o]
    p_buf[q, h] = total

    @pl.when(at_end)
    def _():
        more = p_buf[q, h]
        for o in range(n_slab, 2 * n_slab):
            rcopy(s1_buf.at[o], s1_buf.at[o], s1_ss.at[0], s1_rs.at[o], here).wait_recv()
            more += s1_buf[o]
        p_buf[q, h] = more

    total = p_buf[q, h]
    mine = pl.ds(pl.multiple_of(h * part, 16), part)
    ids = [r_buf[q, k, mine].astype(jnp.float32) for k in range(top)]
    for e in range(n_e):
        m = jnp.zeros((part, 128), jnp.float32)
        for k in range(top):
            m += jnp.where(ids[k] == float(e), total[k], 0.0)
        e_buf[e] = m

    spot = chip * n_h + h
    s2_buf[spot] = e_buf[z]
    n_group = n_chip * n_h
    seconds = []
    for j in range(1, n_group):
        o = lax.rem(spot + j, n_group)
        oc = o // n_h
        oz = lax.rem(oc, n_e)
        c = rcopy(
            e_buf.at[oz], s2_buf.at[spot], s2_ss.at[j - 1], s2_rs.at[spot],
            (g, oc // n_e, oz, lax.rem(o, n_h)),
        )
        c.start()
        seconds.append((o, c))
    cum = cnt_buf[chip]
    for o in others:
        rcopy(cnt_buf.at[o], cnt_buf.at[o], c_ss.at[0], c_rs.at[o], here).wait_recv()
        cum += cnt_buf[o]
    for o, c in seconds:
        rcopy(s2_buf.at[o], s2_buf.at[o], s2_ss.at[0], s2_rs.at[o], here).wait_recv()
    rows = n_group * part
    uv = s2_buf[...].reshape(rows, 128)
    t_buf[...] = uv.T
    cols = k_in // (n_r * n_h)
    ut = t_buf[pl.ds(pl.multiple_of((x * n_h + h) * cols, 8), cols), :]
    pos = lax.broadcasted_iota(jnp.int32, (cols, rows), 1).astype(jnp.float32)
    blocks = []
    for s in range(SEQS):
        keep = pos < cum[s : s + 1, 0:1]
        if s:
            keep &= pos >= cum[s - 1 : s, 0:1]
        blocks.append(jnp.where(keep, ut, 0.0))
    f_buf[...] = lax.dot_general(
        jnp.concatenate(blocks, axis=0), uv, (((1,), (0,)), ((), ())),
        precision=lax.Precision.HIGHEST, preferred_element_type=jnp.float32,
    )
    n_out = SEQS * cols // 2
    even = f_buf[pl.ds(0, n_out, stride=2), :]
    odd = f_buf[pl.ds(1, n_out, stride=2), :]
    out[...] = jnp.where(
        lax.broadcasted_iota(jnp.int32, (n_out, 128), 1) < 64, pltpu.roll(even, 64, 1), odd
    )

    for d, sign in ((0, 1), (1, -1)):
        for step in range(n_e):
            owner = z - sign * step
            for kind in range(4):

                @pl.when((owner >= 0) & (owner < n_e) & takes(kind, z) & takes(kind, z + sign))
                def _():
                    w_copy(kind, owner, z + sign, d).wait_send()

                if step == 0 and kind < 2:

                    @pl.when(at_end & takes(kind, z + sign))
                    def _():
                        w_copy(kind, owner, z + sign, d).wait_send()

    @pl.when(at_end)
    def _():
        for c in ends:
            c.wait_send()

    @pl.when(jnp.logical_not(at_end))
    def _():
        for c in inners + extras:
            c.wait_send()

    for c in sends:
        c.wait_send()
    for _, c in firsts + seconds:
        c.wait_send()


def per_device_fused(sizes, acts, grads, routes, seq_ids, p_in, p_out):
    n_g, n_r, n_e, n_h = sizes
    tok, half_d = acts.shape
    top, half_ff = grads.shape[1], grads.shape[2]
    k_in = p_in.shape[3]
    n_q = n_g * n_r
    da, df = half_d // n_q, half_ff // n_q
    ai, gi = da // 3 // 128 * 128, df * 5 // 16 // 128 * 128
    ent = tok * top
    n_slab, n_chip = n_q * n_h, n_r * n_e
    n_group = n_chip * n_h
    part = tok // n_h
    cols = k_in // (n_r * n_h)
    n_out = SEQS * cols // 2
    bf, f32, dma = jnp.bfloat16, jnp.float32, pltpu.SemaphoreType.DMA
    vmem = pl.BlockSpec(memory_space=pltpu.VMEM)
    hbm = pl.BlockSpec(memory_space=pltpu.HBM)
    features = pl.pallas_call(
        functools.partial(exchange_kernel, sizes),
        out_shape=jax.ShapeDtypeStruct((n_out, 128), f32),
        in_specs=[hbm] * 6,
        out_specs=vmem,
        scratch_shapes=[
            pltpu.VMEM((n_q, tok, da), bf),
            pltpu.VMEM((n_q, tok, top, df), bf),
            pltpu.VMEM((n_q, top, tok, 128), bf),
            pltpu.VMEM((n_e, k_in, da), bf),
            pltpu.VMEM((n_e, k_in, df), bf),
            pltpu.VMEM((n_chip, 8, 128), f32),
            pltpu.VMEM((n_q, n_h, top, part, 128), f32),
            pltpu.VMEM((2 * n_slab, top, part, 128), f32),
            pltpu.VMEM((n_e, part, 128), f32),
            pltpu.VMEM((n_group, part, 128), f32),
            pltpu.VMEM((128, n_group * part), f32),
            pltpu.VMEM((SEQS * cols, 128), f32),
            pltpu.VMEM((n_e // 2, n_q * ent, 128), f32),
            pltpu.VMEM((n_q * ent, df), bf),
            pltpu.VMEM((top, tok), jnp.int32),
            pltpu.VMEM((1, tok), jnp.int32),
            pltpu.VMEM((n_q, tok, ai), bf),
            pltpu.VMEM((n_q, tok, top, gi), bf),
            pltpu.VMEM((n_q, top, tok, 128), bf),
            pltpu.VMEM((n_q, n_h, top, part, 128), f32),
            pltpu.VMEM((n_e // 2, n_q * tok, 128), f32),
            dma((6,)),
            dma((n_q,)), dma((n_q,)), dma((n_q,)), dma((n_q,)), dma((n_q,)), dma((n_q,)),
            dma((4, 2, n_e)), dma((4, n_e)),
            dma((n_chip,)), dma((n_chip,)),
            *[dma((n_q,)) for _ in range(10)], dma((n_slab,)),
            dma((n_slab,)), dma((2 * n_slab,)),
            dma((n_group,)), dma((n_group,)),
        ],
        compiler_params=pltpu.CompilerParams(
            collective_id=0, has_side_effects=True, vmem_limit_bytes=60 * 1024 * 1024
        ),
    )(
        acts,
        grads,
        routes.T,
        seq_ids.reshape(1, tok),
        p_in.reshape(p_in.shape[2], k_in).T,
        p_out.reshape(p_out.shape[2], k_in).T,
    )
    return features.reshape(SEQS, 1, -1)


def fits(sizes):
    n_g, n_r, n_e, n_h = sizes
    return n_g * n_r <= 4 and n_e == 4 and n_h == 2


def solution(mesh):
    sizes = tuple(mesh.shape[name] for name in AXES)
    body = functools.partial(per_device_fused, sizes) if fits(sizes) else per_device
    return jax.shard_map(
        body,
        mesh=mesh,
        in_specs=(
            P(("groups", "rows", "expert"), "pair"),
            P(("groups", "rows", "expert"), None, "pair"),
            P(("groups", "rows", "expert"), None),
            P(("groups", "rows", "expert")),
            P("expert", "pair", "rows", None),
            P("expert", "pair", "rows", None),
        ),
        out_specs=P("groups", "expert", ("rows", "pair")),
        check_vma=False,
    )
```
